128 devices in a mesh: path: 32 (over z, x, core), shard: 4 (over y).
Axes of the slice: x: 4, y: 4, z: 4, core: 2. Of those that a mesh axis runs over, the one named last changes fastest.
Arguments:
- inputs: bfloat16 [65536, 2048], P('path', 'shard'), may hold values from -6 to 6
- out_grad: bfloat16 [65536, 2048], P('path', 'shard'), may hold values from -6 to 6
- path_weights: bfloat16 [32, 2048, 2048], P('path', 'shard'), may hold values from -6 to 6
- inner_drift: float32 [32, 2048, 2048], P('path', 'shard'), may hold values from -4 to 4
- path_module: int32 [32, 1], replicated, may hold values from 0 to 15
- module_slot: int32 [16], replicated, may hold values from 0 to 15, each once
- master: float32 [16, 2048, 2048], P(None, ('shard', 'path')), may hold values from -6 to 6
- momentum: float32 [16, 2048, 2048], P(None, ('shard', 'path')), may hold values from -4 to 4
Outputs:
- input_grad: bfloat16 [65536, 2048], P('path', 'shard')
- new_master: float32 [16, 2048, 2048], P(None, ('shard', 'path'))
- new_momentum: float32 [16, 2048, 2048], P(None, ('shard', 'path'))
- new_weights: bfloat16 [32, 2048, 2048], P('path', 'shard')
The draws below stay inside these ranges and needn't reach their ends.
Inputs may be any that keep to these rules, and one draw needn't show every extreme that they name: `path_module`: every module is used by at least one path. `module_slot`: each slot holds exactly one module.
All inputs are finite; a program needn't handle non-finite values.
Results may differ from the reference program's by a relative error of at most 0.001.
Values may be sent and summed in bfloat16 or wider, within the bound.
No kernel may reach another device: no remote copies, remote signals or barrier semaphores. Data moves between devices by JAX's collectives and lax.ppermute only.
A program may use at most 192 MiB of HBM per device.

```python
import math
import jax
import jax.numpy as jnp
from jax import lax

D = 2048
PATH_TOK = 2048
PATHS = 32
MODULES = 16
TOKENS = 65536


def steps_of(rng, extent, split, least, largest):
    loudness = 1.0
    for dim, blocks in split:
        steps = jax.random.uniform(jax.random.fold_in(jax.random.fold_in(rng, 6), dim), (blocks,), jnp.float32, least / len(split), largest / len(split))
        loudness = loudness * jnp.repeat(jnp.exp(steps), extent[dim] // blocks).reshape((-1,) + (1,) * (len(extent) - 1 - dim))
    return loudness


def different_ones(rng, rows, number_of, top, lift):
    sequence = jax.random.permutation(jax.random.fold_in(rng, 1), number_of)
    pull = sequence
    for power in range(3):
        pull = pull * pull // number_of
    pull = pull * lift // number_of
    chance = jax.random.randint(jax.random.fold_in(rng, 2), (rows, number_of), 0, 4096) + pull
    holders = jax.random.permutation(jax.random.fold_in(rng, 3), rows)[jnp.arange(number_of) % rows]
    chance = jnp.where(jnp.arange(rows)[:, None] == holders[None, :], 1 << 14, chance)
    score = chance * number_of + jnp.arange(number_of)
    return lax.top_k(score.astype(jnp.int32), top)[1].astype(jnp.int32)


def gaussian(rng, dims, spread, limit, cuts=(), held_as=jnp.bfloat16):
    level = steps_of(rng, dims, cuts, -0.22, 0.18) if cuts else 1.0
    drawn = jax.random.normal(rng, dims, jnp.float32) * spread * level
    return jnp.minimum(jnp.maximum(drawn, -limit), limit).astype(held_as)


def setup_inputs(seed: int = 0) -> dict:
    seeds = jax.random.split(jax.random.key(seed), 9)
    return {
        "inputs": gaussian(seeds[0], (TOKENS, D), 1.0, 6.0, ((0, 32), (1, 4))),
        "out_grad": gaussian(seeds[1], (TOKENS, D), 1.0, 6.0, ((0, 32), (1, 4))),
        "path_weights": gaussian(seeds[2], (PATHS, D, D), 1.0, 6.0, ((0, 32), (1, 4))),
        "inner_drift": gaussian(seeds[3], (PATHS, D, D), 0.5, 4.0, ((0, 32), (1, 4)), jnp.float32),
        "path_module": different_ones(seeds[4], PATHS, MODULES, 1, 1024),
        "module_slot": jax.random.permutation(seeds[5], MODULES).astype(jnp.int32),
        "master": gaussian(seeds[6], (MODULES, D, D), 1.0, 6.0, ((1, 128),), jnp.float32),
        "momentum": gaussian(seeds[7], (MODULES, D, D), 0.5, 4.0, ((1, 128),), jnp.float32),
    }


inner_rate = 0.5
outer_rate = 0.7
momentum_coef = 0.9

def reference(inputs, out_grad, path_weights, inner_drift, path_module, module_slot, master, momentum):
    unit_scale = 1.0 / math.sqrt(D)
    path_inputs = inputs.reshape(PATHS, PATH_TOK, D)
    path_grads = out_grad.reshape(PATHS, PATH_TOK, D)
    chosen = path_module[:, 0].astype(jnp.int32)

    def one_path(running, per_path):
        token_rows, grad_rows, weight_rows, drift_rows, module_index = per_path
        grad_full = jnp.dot(token_rows.T, grad_rows, preferred_element_type=jnp.float32) * unit_scale
        back_rows = (jnp.dot(grad_rows, weight_rows.T, preferred_element_type=jnp.float32) * unit_scale).astype(jnp.bfloat16)
        pseudo = drift_rows + inner_rate * grad_full
        running = running.at[module_index].add(pseudo)
        return (running, back_rows)
    start_sums = jnp.zeros((MODULES, D, D), jnp.float32)
    module_sums, back_all = lax.scan(one_path, start_sums, (path_inputs, path_grads, path_weights, inner_drift, chosen))
    member = (chosen[None, :] == jnp.arange(MODULES, dtype=jnp.int32)[:, None]).astype(jnp.float32)
    counts = lax.optimization_barrier(jnp.sum(member, axis=1))
    module_mean = module_sums / counts[:, None, None]
    mean_delta = jnp.zeros_like(master).at[module_slot.astype(jnp.int32)].set(module_mean)
    new_momentum = momentum_coef * momentum + mean_delta
    new_master = master - outer_rate * (mean_delta + momentum_coef * new_momentum)
    slot_of_path = module_slot[chosen].astype(jnp.int32)
    new_weights = new_master[slot_of_path].astype(jnp.bfloat16)
    return (back_all.reshape(TOKENS, D), new_master, new_momentum, new_weights)
```

```python
import math

import jax
import jax.numpy as jnp
from jax import lax
from jax.sharding import PartitionSpec as P

inner_rate = 0.5
outer_rate = 0.7
momentum_coef = 0.9


def ring_gather(block):
    size = lax.axis_size("shard")
    up = [(i, (i + 1) % size) for i in range(size)]
    down = [(i, (i - 1) % size) for i in range(size)]
    half = block.shape[1] // 2
    left = lax.ppermute(block, "shard", up)
    right = lax.ppermute(block, "shard", down)
    far_a = lax.ppermute(left[:, :half], "shard", up)
    far_b = lax.ppermute(right[:, half:], "shard", down)
    return block, left, right, jnp.concatenate([far_a, far_b], axis=1)


def on_device(
    inputs, out_grad, path_weights, inner_drift, path_module, module_slot, master, momentum
):
    path_count = lax.axis_size("path")
    shards = lax.axis_size("shard")
    me = lax.axis_index("shard")
    model_width = path_weights.shape[2]
    width = out_grad.shape[1]
    unit_scale = 1.0 / math.sqrt(model_width)
    blocks = ring_gather(out_grad)
    owners = [me, (me + shards - 1) % shards, (me + 1) % shards, (me + 2) % shards]
    gathered = jnp.zeros((out_grad.shape[0], model_width), out_grad.dtype)
    for block, owner in zip(blocks, owners):
        gathered = lax.dynamic_update_slice(gathered, block, (0, owner * width))

    chosen = path_module[:, 0]
    matches = chosen[:, None] == jnp.arange(module_slot.shape[0], dtype=jnp.int32)[None, :]
    slot_of_path = jnp.sum(jnp.where(matches, module_slot[None, :], 0), axis=1)
    slot_total = master.shape[0]
    member = (slot_of_path[None, :] == jnp.arange(slot_total, dtype=jnp.int32)[:, None]).astype(
        jnp.float32
    )
    counts = jnp.sum(member, axis=1)

    grad_raw = lax.dot_general(
        inputs, gathered, (((0,), (0,)), ((), ())), preferred_element_type=jnp.float32
    )
    pseudo = inner_drift[0] + inner_rate * (grad_raw * unit_scale)
    store_rows = master.shape[1]
    pieces = pseudo.astype(jnp.float16).reshape(path_count, store_rows, model_width)
    received = lax.all_to_all(pieces, "path", split_axis=0, concat_axis=0, tiled=True)
    back_raw = lax.dot_general(
        gathered, path_weights[0], (((1,), (1,)), ((), ())), preferred_element_type=jnp.float32
    )
    input_grad = (back_raw * unit_scale).astype(jnp.bfloat16)

    flattened = received.astype(jnp.float32).reshape(path_count, store_rows * model_width)
    summed = jnp.dot(member, flattened, precision=lax.Precision.HIGHEST)
    slot_sums = summed.reshape(slot_total, store_rows, model_width)
    slot_mean = slot_sums / counts[:, None, None]
    new_momentum = momentum_coef * momentum + slot_mean
    new_master = master - outer_rate * (slot_mean + momentum_coef * new_momentum)
    rounded = new_master.astype(jnp.bfloat16)
    outgoing = jnp.take(rounded, slot_of_path, axis=0)
    back = lax.all_to_all(outgoing, "path", split_axis=0, concat_axis=0, tiled=True)
    new_weights = back.reshape(1, path_count * store_rows, model_width)
    return (input_grad, new_master, new_momentum, new_weights)


def solution(mesh):
    placed = (
        P("path", "shard"),
        P("path", "shard"),
        P("path", "shard", None),
        P("path", "shard", None),
        P(),
        P(),
        P(None, ("shard", "path"), None),
        P(None, ("shard", "path"), None),
    )
    return jax.shard_map(
        on_device,
        mesh=mesh,
        in_specs=placed,
        out_specs=(
            P("path", "shard"),
            P(None, ("shard", "path"), None),
            P(None, ("shard", "path"), None),
            P("path", "shard", None),
        ),
        check_vma=False,
    )
```

```python
import functools
import math

import jax
import jax.numpy as jnp
from jax import lax
from jax.experimental import pallas as pl
from jax.experimental.pallas import tpu as pltpu
from jax.sharding import PartitionSpec as P

inner_rate = 0.5
outer_rate = 0.7
momentum_coef = 0.9
pseudo_lift = 64.0
weight_lift = 32.0
kernel_vmem = 60 * 1024 * 1024


def update_kernel(slots, blocks, shares, rec, master, momentum, *refs):
    new_master, new_momentum, outgoing, total = refs[-4:]
    paths, slot_total = rec.shape[0], master.shape[0]
    total[...] = jnp.zeros_like(total)
    for p in range(paths):
        total[slots[p]] += rec[p]
    for m in range(slot_total):
        mean = total[m] * shares[m]
        moved = momentum_coef * momentum[m] + mean
        new_momentum[m] = moved
        new_master[m] = master[m] - outer_rate * (mean + momentum_coef * moved)
    for p in range(paths):
        outgoing[p] = new_master[slots[p]].astype(outgoing.dtype)


def update(slots, blocks, shares, rec, master, momentum, out_width, first, earlier):
    paths, rows, width = rec.shape
    slot_total = master.shape[0]
    block = width // blocks.shape[0]
    unit = block // 2
    skipped = first // unit
    held = pl.BlockSpec((slot_total, rows, unit), lambda j, k, s, u, c: (0, 0, 2 * u[j] + k))
    passing = pl.BlockSpec((paths, rows, unit), lambda j, k, s, u, c: (0, 0, 2 * j + k))
    leaving = pl.BlockSpec((paths, rows, unit), lambda j, k, s, u, c: (0, 0, skipped + 2 * j + k))
    whole = pl.BlockSpec(memory_space=pl.ANY)
    return pl.pallas_call(
        update_kernel,
        grid_spec=pltpu.PrefetchScalarGridSpec(
            num_scalar_prefetch=3,
            grid=(blocks.shape[0], 2),
            in_specs=[passing, held, held] + [whole] * len(earlier),
            out_specs=[held, held, leaving],
            scratch_shapes=[pltpu.VMEM((slot_total, rows, unit), jnp.float32)],
        ),
        out_shape=[
            jax.ShapeDtypeStruct(master.shape, master.dtype),
            jax.ShapeDtypeStruct(momentum.shape, momentum.dtype),
            jax.ShapeDtypeStruct((paths, rows, out_width), jnp.bfloat16),
        ],
        input_output_aliases={6 + i: i for i in range(len(earlier))},
        compiler_params=pltpu.CompilerParams(vmem_limit_bytes=kernel_vmem),
        cost_estimate=pl.CostEstimate(
            flops=4 * rec.size,
            bytes_accessed=6 * rec.size + 16 * slot_total * rows * width,
            transcendentals=0,
        ),
    )(slots, blocks, shares, rec, master, momentum, *earlier)


def place_kernel(orders, which, *refs):
    *pieces, out = refs
    width = out.shape[1] // len(orders[0])
    for choice, order in enumerate(orders):

        @pl.when(which[0] == choice)
        def _():
            k = 0
            for piece in pieces:
                for i in range(piece.shape[1] // width):
                    first = order[k] * width
                    out[:, first : first + width] = piece[:, i * width : (i + 1) * width]
                    k += 1


def place(orders, which, pieces):
    rows, width = pieces[0].shape
    whole = len(orders[0]) * width
    tile = min(rows, 128)
    return pl.pallas_call(
        functools.partial(place_kernel, orders),
        grid_spec=pltpu.PrefetchScalarGridSpec(
            num_scalar_prefetch=1,
            grid=(rows // tile,),
            in_specs=[pl.BlockSpec((tile, p.shape[1]), lambda i, u: (i, 0)) for p in pieces],
            out_specs=pl.BlockSpec((tile, whole), lambda i, u: (i, 0)),
        ),
        out_shape=jax.ShapeDtypeStruct((rows, whole), pieces[0].dtype),
        compiler_params=pltpu.CompilerParams(vmem_limit_bytes=kernel_vmem),
        cost_estimate=pl.CostEstimate(
            flops=0, bytes_accessed=4 * rows * whole, transcendentals=0
        ),
    )(which, *pieces)


def back_kernel(scale, starts, weights, *refs):
    out = refs[-1]
    total = jnp.zeros(out.shape, jnp.float32)
    for i, block in enumerate(refs[:-1]):
        depth = block.shape[1]
        first = pl.multiple_of(starts[i], depth)
        total += jnp.dot(
            block[...], weights[pl.ds(first, depth), :], preferred_element_type=jnp.float32
        )
    out[...] = (total * scale).astype(out.dtype)


def input_gradient(blocks, starts, weights, scale):
    tokens = blocks[0].shape[0]
    model_width, width = weights.shape
    tile = min(tokens, 512)
    return pl.pallas_call(
        functools.partial(back_kernel, scale),
        grid_spec=pltpu.PrefetchScalarGridSpec(
            num_scalar_prefetch=1,
            grid=(tokens // tile,),
            in_specs=[pl.BlockSpec((model_width, width), lambda i, u: (0, 0))]
            + [pl.BlockSpec((tile, b.shape[1]), lambda i, u: (i, 0)) for b in blocks],
            out_specs=pl.BlockSpec((tile, width), lambda i, u: (i, 0)),
        ),
        out_shape=jax.ShapeDtypeStruct((tokens, width), jnp.bfloat16),
        compiler_params=pltpu.CompilerParams(vmem_limit_bytes=kernel_vmem),
        cost_estimate=pl.CostEstimate(
            flops=2 * tokens * model_width * width,
            bytes_accessed=2 * (tokens * model_width + model_width * width + tokens * width),
            transcendentals=0,
        ),
    )(starts, weights, *blocks)


def on_device(
    inputs, out_grad, path_weights, inner_drift, path_module, module_slot, master, momentum
):
    paths = lax.axis_size("path")
    size = lax.axis_size("shard")
    me = lax.axis_index("shard")
    model_width = path_weights.shape[2]
    width = out_grad.shape[1]
    half = width // 2
    rows = master.shape[1]
    slot_total = master.shape[0]
    unit_scale = 1.0 / math.sqrt(model_width)

    here, left, right, far = me, (me + size - 1) % size, (me + 1) % size, (me + 2) % size
    odd = lax.axis_index("path") % 2

    def stepped(block, sense):
        return lax.ppermute(
            block,
            ("path", "shard"),
            [
                (p * size + y, p * size + (y + (sense if p % 2 == 0 else -sense)) % size)
                for p in range(paths)
                for y in range(size)
            ],
        )

    chosen = path_module[:, 0]
    matches = chosen[:, None] == jnp.arange(module_slot.shape[0], dtype=jnp.int32)[None, :]
    slots = jnp.sum(jnp.where(matches, module_slot[None, :], 0), axis=1)
    shares = 1.0 / jnp.sum(
        (slots[None, :] == jnp.arange(slot_total, dtype=jnp.int32)[:, None]).astype(jnp.float32),
        axis=1,
    )

    drift = inner_drift[0]
    turned_inputs = lax.optimization_barrier(inputs.T)

    def pseudo_pieces(block, first):
        columns = block.shape[1]
        raw = jnp.dot(turned_inputs, block, preferred_element_type=jnp.float32)
        moved = lax.dynamic_slice(drift, (0, first), (drift.shape[0], columns))
        value = (moved + inner_rate * (raw * unit_scale)) * pseudo_lift
        return value.astype(jnp.float16).reshape(paths, rows, columns)

    def exchange(parts):
        whole = parts[0] if len(parts) == 1 else jnp.concatenate(parts, axis=2)
        return lax.all_to_all(whole, "path", split_axis=0, concat_axis=0, tiled=True)

    def updated(got, blocks, out_width, first, earlier):
        rec = got.astype(jnp.float32) * (1.0 / pseudo_lift)
        order = jnp.stack(blocks).astype(jnp.int32)
        return update(slots, order, shares, rec, master, momentum, out_width, first, earlier)

    first_block = stepped(out_grad, 1)
    second_block = stepped(out_grad, -1)
    got = exchange([pseudo_pieces(out_grad, here * width)])
    *earlier, outgoing = updated(got, [here], width, 0, [])
    own_sent = exchange([outgoing]).reshape(paths * rows, width)
    first_block, second_block, own_sent = lax.optimization_barrier(
        (first_block, second_block, own_sent)
    )
    far_block = stepped(first_block, 1)

    first, second = jnp.where(odd == 0, left, right), jnp.where(odd == 0, right, left)
    got = exchange(
        [pseudo_pieces(first_block, first * width), pseudo_pieces(second_block, second * width)]
    )
    even_path = (jnp.arange(paths) % 2 == 0)[:, None, None]
    left_got = jnp.where(even_path, got[:, :, :width], got[:, :, width:])
    right_got = jnp.where(even_path, got[:, :, width:], got[:, :, :width])
    *earlier, outgoing = updated(
        jnp.concatenate([left_got, right_got], axis=2), [left, right], 3 * width, 0, earlier
    )
    got = exchange([pseudo_pieces(far_block, far * width)])
    new_master, new_momentum, outgoing = updated(
        got, [far], 3 * width, 2 * width, [*earlier, outgoing]
    )
    sent = exchange([outgoing]).reshape(paths * rows, 3 * width)
    orders = [[(i + d) % size for d in (0, size - 1, 1, 2)] for i in range(size)]
    new_weights = place(orders, me.astype(jnp.int32)[None], [own_sent, sent])

    turned_weights = path_weights[0].T
    blocks = [out_grad, first_block, second_block, far_block]
    starts = jnp.stack([here, first, second, far]).astype(jnp.int32) * width
    input_grad = input_gradient(blocks, starts, turned_weights, unit_scale)
    return (input_grad, new_master, new_momentum, new_weights[None])


def solution(mesh):
    placed = (
        P("path", "shard"),
        P("path", "shard"),
        P("path", "shard", None),
        P("path", "shard", None),
        P(),
        P(),
        P(None, ("shard", "path"), None),
        P(None, ("shard", "path"), None),
    )
    return jax.shard_map(
        on_device,
        mesh=mesh,
        in_specs=placed,
        out_specs=(
            P("path", "shard"),
            P(None, ("shard", "path"), None),
            P(None, ("shard", "path"), None),
            P("path", "shard", None),
        ),
        check_vma=False,
    )
```

```python
import functools
import math

import jax
import jax.numpy as jnp
from jax import lax
from jax.experimental import pallas as pl
from jax.experimental.pallas import tpu as pltpu
from jax.sharding import PartitionSpec as P

inner_rate = 0.5
outer_rate = 0.7
momentum_coef = 0.9
pseudo_lift = 64.0
weight_lift = 32.0
kernel_vmem = 24 * 1024 * 1024
small_vmem = 10 * 1024 * 1024


def update_kernel(slots, blocks, shares, rec, master, momentum, *refs):
    new_master, new_momentum, outgoing, total = refs[-4:]
    paths, slot_total = rec.shape[0], master.shape[0]
    total[...] = jnp.zeros_like(total)
    for p in range(paths):
        total[slots[p]] += rec[p]
    for m in range(slot_total):
        mean = total[m] * shares[m]
        moved = momentum_coef * momentum[m] + mean
        new_momentum[m] = moved
        new_master[m] = master[m] - outer_rate * (mean + momentum_coef * moved)
    for p in range(paths):
        outgoing[p] = new_master[slots[p]].astype(outgoing.dtype)


def update(slots, blocks, shares, rec, master, momentum, earlier, out_width, first):
    paths, rows, width = rec.shape
    slot_total = master.shape[0]
    unit = width // blocks.shape[0] // 2
    skipped = first // unit
    held = pl.BlockSpec((slot_total, rows, unit), lambda j, k, s, u, c: (0, 0, 2 * u[j] + k))
    passing = pl.BlockSpec((paths, rows, unit), lambda j, k, s, u, c: (0, 0, 2 * j + k))
    leaving = pl.BlockSpec((paths, rows, unit), lambda j, k, s, u, c: (0, 0, skipped + 2 * j + k))
    whole = pl.BlockSpec(memory_space=pl.ANY)
    master, momentum, *earlier = [
        pltpu.with_memory_space_constraint(x, pltpu.HBM) for x in (master, momentum, *earlier)
    ]
    return pl.pallas_call(
        update_kernel,
        grid_spec=pltpu.PrefetchScalarGridSpec(
            num_scalar_prefetch=3,
            grid=(blocks.shape[0], 2),
            in_specs=[passing, held, held] + [whole] * len(earlier),
            out_specs=[held, held, leaving],
            scratch_shapes=[pltpu.VMEM((slot_total, rows, unit), jnp.float32)],
        ),
        out_shape=[
            pltpu.HBM(master.shape, master.dtype),
            pltpu.HBM(momentum.shape, momentum.dtype),
            pltpu.HBM((paths, rows, out_width), jnp.bfloat16),
        ],
        input_output_aliases={6 + i: i for i in range(len(earlier))},
        compiler_params=pltpu.CompilerParams(vmem_limit_bytes=small_vmem),
        cost_estimate=pl.CostEstimate(
            flops=4 * rec.size,
            bytes_accessed=6 * rec.size + 16 * slot_total * rows * width,
            transcendentals=0,
        ),
    )(slots, blocks, shares, rec, master, momentum, *earlier)


def place_kernel(orders, which, *refs):
    *pieces, out = refs
    width = out.shape[1] // len(orders[0])
    for choice, order in enumerate(orders):

        @pl.when(which[0] == choice)
        def _():
            k = 0
            for piece in pieces:
                for i in range(piece.shape[1] // width):
                    first = order[k] * width
                    out[:, first : first + width] = piece[:, i * width : (i + 1) * width]
                    k += 1


def place(orders, which, pieces):
    rows, width = pieces[0].shape
    whole = len(orders[0]) * width
    tile = rows // 2
    return pl.pallas_call(
        functools.partial(place_kernel, orders),
        grid_spec=pltpu.PrefetchScalarGridSpec(
            num_scalar_prefetch=1,
            grid=(rows // tile,),
            in_specs=[pl.BlockSpec((tile, p.shape[1]), lambda i, u: (i, 0)) for p in pieces],
            out_specs=pl.BlockSpec((tile, whole), lambda i, u: (i, 0)),
        ),
        out_shape=jax.ShapeDtypeStruct((rows, whole), pieces[0].dtype),
        compiler_params=pltpu.CompilerParams(vmem_limit_bytes=kernel_vmem),
        cost_estimate=pl.CostEstimate(
            flops=0, bytes_accessed=4 * rows * whole, transcendentals=0
        ),
    )(which, *pieces)


def back_kernel(scale, starts, weights, *refs):
    out = refs[-1]
    total = jnp.zeros(out.shape, jnp.float32)
    for i, block in enumerate(refs[:-1]):
        depth = block.shape[1]
        first = pl.multiple_of(starts[i], depth)
        total += jnp.dot(
            block[...], weights[pl.ds(first, depth), :], preferred_element_type=jnp.float32
        )
    out[...] = (total * scale).astype(out.dtype)


def input_gradient(blocks, starts, weights, scale):
    tokens = blocks[0].shape[0]
    model_width, width = weights.shape
    tile = min(tokens, 512)
    return pl.pallas_call(
        functools.partial(back_kernel, scale),
        grid_spec=pltpu.PrefetchScalarGridSpec(
            num_scalar_prefetch=1,
            grid=(tokens // tile,),
            in_specs=[pl.BlockSpec((model_width, width), lambda i, u: (0, 0))]
            + [pl.BlockSpec((tile, b.shape[1]), lambda i, u: (i, 0)) for b in blocks],
            out_specs=pl.BlockSpec((tile, width), lambda i, u: (i, 0)),
        ),
        out_shape=jax.ShapeDtypeStruct((tokens, width), jnp.bfloat16),
        compiler_params=pltpu.CompilerParams(vmem_limit_bytes=kernel_vmem),
        cost_estimate=pl.CostEstimate(
            flops=2 * tokens * model_width * width,
            bytes_accessed=2 * (tokens * model_width + model_width * width + tokens * width),
            transcendentals=0,
        ),
    )(starts, weights, *blocks)


def on_device(
    inputs, out_grad, path_weights, inner_drift, path_module, module_slot, master, momentum
):
    paths = lax.axis_size("path")
    size = lax.axis_size("shard")
    me = lax.axis_index("shard")
    model_width = path_weights.shape[2]
    width = out_grad.shape[1]
    half = width // 2
    rows = master.shape[1]
    slot_total = master.shape[0]
    unit_scale = 1.0 / math.sqrt(model_width)

    here, left, right, far = me, (me + size - 1) % size, (me + 1) % size, (me + 2) % size
    odd = lax.axis_index("path") % 2

    def stepped(block, sense):
        return lax.ppermute(
            block,
            ("path", "shard"),
            [
                (p * size + y, p * size + (y + (sense if p % 2 == 0 else -sense)) % size)
                for p in range(paths)
                for y in range(size)
            ],
        )

    chosen = path_module[:, 0]
    matches = chosen[:, None] == jnp.arange(module_slot.shape[0], dtype=jnp.int32)[None, :]
    slots = jnp.sum(jnp.where(matches, module_slot[None, :], 0), axis=1)
    shares = 1.0 / jnp.sum(
        (slots[None, :] == jnp.arange(slot_total, dtype=jnp.int32)[:, None]).astype(jnp.float32),
        axis=1,
    )

    drift = inner_drift[0]
    turned_inputs = lax.optimization_barrier(inputs.T)

    def pseudo_pieces(block, first):
        columns = block.shape[1]
        raw = jnp.dot(turned_inputs, block, preferred_element_type=jnp.float32)
        moved = lax.dynamic_slice(drift, (0, first), (drift.shape[0], columns))
        value = (moved + inner_rate * (raw * unit_scale)) * pseudo_lift
        return value.astype(jnp.float16).reshape(paths, rows, columns)

    def exchange(parts):
        whole = parts[0] if len(parts) == 1 else jnp.concatenate(parts, axis=2)
        return lax.all_to_all(whole, "path", split_axis=0, concat_axis=0, tiled=True)

    def updated(got, blocks, earlier, out_width, first=0):
        rec = got.astype(jnp.float32) * (1.0 / pseudo_lift)
        order = jnp.stack(blocks).astype(jnp.int32)
        return update(slots, order, shares, rec, master, momentum, earlier, out_width, first)

    first_block = stepped(out_grad, 1)
    second_block = stepped(out_grad, -1)
    got = exchange([pseudo_pieces(out_grad, here * width)])
    *earlier, outgoing = updated(got, [here], [], width)
    own_sent = exchange([outgoing]).reshape(paths * rows, width)
    first_block, second_block, own_sent = lax.optimization_barrier(
        (first_block, second_block, own_sent)
    )
    far_block = stepped(first_block, 1)

    first, second = jnp.where(odd == 0, left, right), jnp.where(odd == 0, right, left)
    got = exchange(
        [pseudo_pieces(first_block, first * width), pseudo_pieces(second_block, second * width)]
    )
    far_pieces = pseudo_pieces(far_block, far * width)
    got, far_pieces = lax.optimization_barrier((got, far_pieces))
    far_got = exchange([far_pieces])
    even_path = (jnp.arange(paths) % 2 == 0)[:, None, None]
    left_got = jnp.where(even_path, got[:, :, :width], got[:, :, width:])
    right_got = jnp.where(even_path, got[:, :, width:], got[:, :, :width])
    *earlier, outgoing = updated(
        jnp.concatenate([left_got, right_got], axis=2), [left, right], earlier, 3 * width
    )
    new_master, new_momentum, outgoing = updated(
        far_got, [far], [*earlier, outgoing], 3 * width, 2 * width
    )
    sent = exchange([outgoing]).reshape(paths * rows, 3 * width)

    blocks = [out_grad, first_block, second_block, far_block]
    starts = jnp.stack([here, first, second, far]).astype(jnp.int32) * width
    input_grad = input_gradient(blocks, starts, path_weights[0].T, unit_scale)
    sent, new_master, new_momentum, input_grad = lax.optimization_barrier(
        (sent, new_master, new_momentum, input_grad)
    )
    orders = [[(i + d) % size for d in (0, size - 1, 1, 2)] for i in range(size)]
    new_weights = place(orders, me.astype(jnp.int32)[None], [own_sent, sent])
    return (input_grad, new_master, new_momentum, new_weights[None])


def solution(mesh):
    placed = (
        P("path", "shard"),
        P("path", "shard"),
        P("path", "shard", None),
        P("path", "shard", None),
        P(),
        P(),
        P(None, ("shard", "path"), None),
        P(None, ("shard", "path"), None),
    )
    return jax.shard_map(
        on_device,
        mesh=mesh,
        in_specs=placed,
        out_specs=(
            P("path", "shard"),
            P(None, ("shard", "path"), None),
            P(None, ("shard", "path"), None),
            P("path", "shard", None),
        ),
        check_vma=False,
    )
```

```python
import functools
import math

import jax
import jax.numpy as jnp
from jax import lax
from jax.experimental import pallas as pl
from jax.experimental.pallas import tpu as pltpu
from jax.sharding import PartitionSpec as P

inner_rate = 0.5
outer_rate = 0.7
momentum_coef = 0.9
pseudo_lift = 64.0
weight_lift = 32.0
kernel_vmem = 24 * 1024 * 1024
small_vmem = 10 * 1024 * 1024


def update_kernel(stores, passes_on, slots, blocks, shares, rec, master, momentum, *refs):
    *results, total = refs[-(2 * stores + passes_on + 1) :]
    paths, slot_total = rec.shape[0], master.shape[0]
    total[...] = jnp.zeros_like(total)
    for p in range(paths):
        total[slots[p]] += rec[p]
    for m in range(slot_total):
        mean = total[m] * shares[m]
        moved = momentum_coef * momentum[m] + mean
        fresh = master[m] - outer_rate * (mean + momentum_coef * moved)
        total[m] = fresh
        if stores:
            results[0][m] = fresh
            results[1][m] = moved
    if passes_on:
        for p in range(paths):
            results[-1][p] = total[slots[p]].astype(results[-1].dtype)


def update(slots, blocks, shares, rec, master, momentum, earlier, out_width=0, first=0, stores=True):
    paths, rows, width = rec.shape
    slot_total = master.shape[0]
    unit = width // blocks.shape[0] // 2
    skipped = first // unit
    held = pl.BlockSpec((slot_total, rows, unit), lambda j, k, s, u, c: (0, 0, 2 * u[j] + k))
    passing = pl.BlockSpec((paths, rows, unit), lambda j, k, s, u, c: (0, 0, 2 * j + k))
    leaving = pl.BlockSpec((paths, rows, unit), lambda j, k, s, u, c: (0, 0, skipped + 2 * j + k))
    whole = pl.BlockSpec(memory_space=pl.ANY)
    results = [pltpu.HBM(x.shape, x.dtype) for x in (master, momentum)] if stores else []
    if out_width:
        results.append(pltpu.HBM((paths, rows, out_width), jnp.bfloat16))
    master, momentum, *earlier = [
        pltpu.with_memory_space_constraint(x, pltpu.HBM) for x in (master, momentum, *earlier)
    ]
    return pl.pallas_call(
        functools.partial(update_kernel, stores, out_width > 0),
        grid_spec=pltpu.PrefetchScalarGridSpec(
            num_scalar_prefetch=3,
            grid=(blocks.shape[0], 2),
            in_specs=[passing, held, held] + [whole] * len(earlier),
            out_specs=[held] * (2 * stores) + [leaving] * (out_width > 0),
            scratch_shapes=[pltpu.VMEM((slot_total, rows, unit), jnp.float32)],
        ),
        out_shape=results,
        input_output_aliases={6 + i: i for i in range(len(earlier))},
        compiler_params=pltpu.CompilerParams(vmem_limit_bytes=small_vmem),
        cost_estimate=pl.CostEstimate(
            flops=4 * rec.size,
            bytes_accessed=6 * rec.size + 16 * slot_total * rows * width,
            transcendentals=0,
        ),
    )(slots, blocks, shares, rec, master, momentum, *earlier)


def last_update_kernel(first, slots, blocks, shares, rec, master, momentum, *refs):
    new_master, new_momentum, outgoing, fresh, moved, leaving, sent = refs[3:]
    paths, slot_total, width = rec.shape[0], master.shape[0], rec.shape[2]
    unit = width // 2
    start = pl.multiple_of(blocks[0] * width, width)
    copies = []
    for k in range(2):
        cut = slice(k * unit, (k + 1) * unit)
        fresh[:, :, cut] = jnp.zeros((slot_total, rec.shape[1], unit), jnp.float32)
        for p in range(paths):
            fresh[slots[p], :, cut] += rec[p, :, cut]
        for m in range(slot_total):
            mean = fresh[m, :, cut] * shares[m]
            moved[m, :, cut] = momentum_coef * momentum[m, :, cut] + mean
            fresh[m, :, cut] = master[m, :, cut] - outer_rate * (
                mean + momentum_coef * moved[m, :, cut]
            )
        for p in range(paths):
            leaving[p, :, cut] = fresh[slots[p], :, cut].astype(leaving.dtype)
        for source, target, place in (
            (leaving, outgoing, first + k * unit),
            (fresh, new_master, start + k * unit),
            (moved, new_momentum, start + k * unit),
        ):
            here = pl.ds(pl.multiple_of(place, unit), unit)
            copies.append(
                pltpu.make_async_copy(
                    source.at[:, :, cut], target.at[:, :, here], sent.at[len(copies)]
                )
            )
            copies[-1].start()
    for copy in copies:
        copy.wait()


def last_update(slots, blocks, shares, rec, master, momentum, earlier, first):
    block = (master.shape[0], rec.shape[1], rec.shape[2])
    number, inside = (pl.BlockSpec(memory_space=m) for m in (pltpu.SMEM, pltpu.VMEM))
    whole = pl.BlockSpec(memory_space=pl.ANY)
    rec, master, momentum = [
        pltpu.with_memory_space_constraint(x, pltpu.VMEM) for x in (rec, master, momentum)
    ]
    earlier = [pltpu.with_memory_space_constraint(x, pltpu.HBM) for x in earlier]
    return pl.pallas_call(
        functools.partial(last_update_kernel, first),
        in_specs=[number] * 3 + [inside] * 3 + [whole] * 3,
        out_specs=[whole] * 3,
        out_shape=[pltpu.HBM(x.shape, x.dtype) for x in earlier],
        scratch_shapes=[
            pltpu.VMEM(block, jnp.float32),
            pltpu.VMEM(block, jnp.float32),
            pltpu.VMEM(rec.shape, jnp.bfloat16),
            pltpu.SemaphoreType.DMA((6,)),
        ],
        input_output_aliases={6 + i: i for i in range(3)},
        compiler_params=pltpu.CompilerParams(vmem_limit_bytes=small_vmem),
        cost_estimate=pl.CostEstimate(
            flops=4 * rec.size, bytes_accessed=8 * rec.size, transcendentals=0
        ),
    )(slots, blocks, shares, rec, master, momentum, *earlier)


def place_kernel(orders, which, *refs):
    *pieces, out = refs
    width = out.shape[1] // len(orders[0])
    for choice, order in enumerate(orders):

        @pl.when(which[0] == choice)
        def _():
            k = 0
            for piece in pieces:
                for i in range(piece.shape[1] // width):
                    first = order[k] * width
                    out[:, first : first + width] = piece[:, i * width : (i + 1) * width]
                    k += 1


def place(orders, which, pieces):
    rows, width = pieces[0].shape
    whole = len(orders[0]) * width
    pieces = [pltpu.with_memory_space_constraint(piece, pltpu.HBM) for piece in pieces]
    tile = rows // 2
    return pl.pallas_call(
        functools.partial(place_kernel, orders),
        grid_spec=pltpu.PrefetchScalarGridSpec(
            num_scalar_prefetch=1,
            grid=(rows // tile,),
            in_specs=[pl.BlockSpec((tile, p.shape[1]), lambda i, u: (i, 0)) for p in pieces],
            out_specs=pl.BlockSpec((tile, whole), lambda i, u: (i, 0)),
        ),
        out_shape=jax.ShapeDtypeStruct((rows, whole), pieces[0].dtype),
        compiler_params=pltpu.CompilerParams(vmem_limit_bytes=kernel_vmem),
        cost_estimate=pl.CostEstimate(
            flops=0, bytes_accessed=4 * rows * whole, transcendentals=0
        ),
    )(which, *pieces)


def back_kernel(scale, starts, weights, *refs):
    out = refs[-1]
    total = jnp.zeros(out.shape, jnp.float32)
    for i, block in enumerate(refs[:-1]):
        depth = block.shape[1]
        first = pl.multiple_of(starts[i], depth)
        total += jnp.dot(
            block[...], weights[pl.ds(first, depth), :], preferred_element_type=jnp.float32
        )
    out[...] = (total * scale).astype(out.dtype)


def input_gradient(blocks, starts, weights, scale):
    tokens = blocks[0].shape[0]
    model_width, width = weights.shape
    tile = min(tokens, 512)
    return pl.pallas_call(
        functools.partial(back_kernel, scale),
        grid_spec=pltpu.PrefetchScalarGridSpec(
            num_scalar_prefetch=1,
            grid=(tokens // tile,),
            in_specs=[pl.BlockSpec((model_width, width), lambda i, u: (0, 0))]
            + [pl.BlockSpec((tile, b.shape[1]), lambda i, u: (i, 0)) for b in blocks],
            out_specs=pl.BlockSpec((tile, width), lambda i, u: (i, 0)),
        ),
        out_shape=jax.ShapeDtypeStruct((tokens, width), jnp.bfloat16),
        compiler_params=pltpu.CompilerParams(vmem_limit_bytes=kernel_vmem),
        cost_estimate=pl.CostEstimate(
            flops=2 * tokens * model_width * width,
            bytes_accessed=2 * (tokens * model_width + model_width * width + tokens * width),
            transcendentals=0,
        ),
    )(starts, weights, *blocks)


def on_device(
    inputs, out_grad, path_weights, inner_drift, path_module, module_slot, master, momentum
):
    paths = lax.axis_size("path")
    size = lax.axis_size("shard")
    me = lax.axis_index("shard")
    model_width = path_weights.shape[2]
    width = out_grad.shape[1]
    half = width // 2
    rows = master.shape[1]
    slot_total = master.shape[0]
    unit_scale = 1.0 / math.sqrt(model_width)

    here, left, right, far = me, (me + size - 1) % size, (me + 1) % size, (me + 2) % size
    odd = lax.axis_index("path") % 2

    def stepped(block, sense):
        return lax.ppermute(
            block,
            ("path", "shard"),
            [
                (p * size + y, p * size + (y + (sense if p % 2 == 0 else -sense)) % size)
                for p in range(paths)
                for y in range(size)
            ],
        )

    chosen = path_module[:, 0]
    matches = chosen[:, None] == jnp.arange(module_slot.shape[0], dtype=jnp.int32)[None, :]
    slots = jnp.sum(jnp.where(matches, module_slot[None, :], 0), axis=1)
    shares = 1.0 / jnp.sum(
        (slots[None, :] == jnp.arange(slot_total, dtype=jnp.int32)[:, None]).astype(jnp.float32),
        axis=1,
    )

    drift = inner_drift[0]
    turned_inputs = lax.optimization_barrier(inputs.T)

    def drift_columns(block):
        return lax.dynamic_slice(drift, (0, block * width), (drift.shape[0], width))

    def pseudo_pieces(block, moved):
        raw = jnp.dot(turned_inputs, block, preferred_element_type=jnp.float32)
        value = (moved + inner_rate * (raw * unit_scale)) * pseudo_lift
        return value.astype(jnp.float16).reshape(paths, rows, width)

    def exchange(pieces):
        return lax.all_to_all(pieces, "path", split_axis=0, concat_axis=0, tiled=True)

    def received(got):
        return got.astype(jnp.float32) * (1.0 / pseudo_lift)

    def updated(rec, blocks, earlier, **choice):
        order = jnp.stack(blocks).astype(jnp.int32)
        return update(slots, order, shares, rec, master, momentum, earlier, **choice)

    first_block = stepped(out_grad, 1)
    pieces = pseudo_pieces(out_grad, drift_columns(here))
    pieces, late_grad = lax.optimization_barrier((pieces, out_grad))
    second_block = stepped(late_grad, -1)
    got = exchange(pieces)
    *earlier, outgoing = updated(received(got), [here], [], out_width=width)
    own_sent = exchange(outgoing).reshape(paths * rows, width)
    first, second = jnp.where(odd == 0, left, right), jnp.where(odd == 0, right, left)
    far_store = [
        lax.dynamic_slice(store, (0, 0, far * width), (slot_total, rows, width))
        for store in (master, momentum)
    ]
    first_block, own_sent, far_store = lax.optimization_barrier((first_block, own_sent, far_store))
    first_pieces = pseudo_pieces(first_block, drift_columns(first))
    first_block, first_pieces = lax.optimization_barrier((first_block, first_pieces))
    far_block = stepped(first_block, 1)

    second_pieces = pseudo_pieces(second_block, drift_columns(second))
    got = exchange(jnp.concatenate([first_pieces, second_pieces], axis=2))
    far_pieces = pseudo_pieces(far_block, drift_columns(far))
    got, far_pieces = lax.optimization_barrier((got, far_pieces))
    far_got = exchange(far_pieces)
    even_path = (jnp.arange(paths) % 2 == 0)[:, None, None]
    left_got = jnp.where(even_path, got[:, :, :width], got[:, :, width:])
    right_got = jnp.where(even_path, got[:, :, width:], got[:, :, :width])
    *earlier, outgoing = updated(
        received(jnp.concatenate([left_got, right_got], axis=2)),
        [left, right],
        earlier,
        out_width=3 * width,
    )
    new_master, new_momentum, outgoing = last_update(
        slots,
        far.astype(jnp.int32)[None],
        shares,
        received(far_got),
        *far_store,
        [*earlier, outgoing],
        2 * width,
    )
    sent = exchange(outgoing).reshape(paths * rows, 3 * width)

    blocks = [out_grad, first_block, second_block, far_block]
    starts = jnp.stack([here, first, second, far]).astype(jnp.int32) * width
    input_grad = input_gradient(blocks, starts, path_weights[0].T, unit_scale)
    sent, new_master, new_momentum, input_grad = lax.optimization_barrier(
        (sent, new_master, new_momentum, input_grad)
    )
    orders = [[(i + d) % size for d in (0, size - 1, 1, 2)] for i in range(size)]
    new_weights = place(orders, me.astype(jnp.int32)[None], [own_sent, sent])
    return (input_grad, new_master, new_momentum, new_weights[None])


def solution(mesh):
    placed = (
        P("path", "shard"),
        P("path", "shard"),
        P("path", "shard", None),
        P("path", "shard", None),
        P(),
        P(),
        P(None, ("shard", "path"), None),
        P(None, ("shard", "path"), None),
    )
    return jax.shard_map(
        on_device,
        mesh=mesh,
        in_specs=placed,
        out_specs=(
            P("path", "shard"),
            P(None, ("shard", "path"), None),
            P(None, ("shard", "path"), None),
            P("path", "shard", None),
        ),
        check_vma=False,
    )
```

```python
import functools
import math

import jax
import jax.numpy as jnp
from jax import lax
from jax.experimental import pallas as pl
from jax.experimental.pallas import tpu as pltpu
from jax.sharding import PartitionSpec as P

inner_rate = 0.5
outer_rate = 0.7
momentum_coef = 0.9
pseudo_lift = 64.0
weight_lift = 32.0
kernel_vmem = 24 * 1024 * 1024
small_vmem = 10 * 1024 * 1024


def update_kernel(stores, passes_on, slots, blocks, shares, rec, master, momentum, *refs):
    *results, total = refs[-(2 * stores + passes_on + 1) :]
    paths, slot_total = rec.shape[0], master.shape[0]
    total[...] = jnp.zeros_like(total)
    for p in range(paths):
        total[slots[p]] += rec[p]
    for m in range(slot_total):
        mean = total[m] * shares[m]
        moved = momentum_coef * momentum[m] + mean
        fresh = master[m] - outer_rate * (mean + momentum_coef * moved)
        total[m] = fresh
        if stores:
            results[0][m] = fresh
            results[1][m] = moved
    if passes_on:
        for p in range(paths):
            results[-1][p] = total[slots[p]].astype(results[-1].dtype)


def update(slots, blocks, shares, rec, master, momentum, earlier, out_width=0, first=0, stores=True):
    paths, rows, width = rec.shape
    slot_total = master.shape[0]
    unit = width // blocks.shape[0] // 2
    skipped = first // unit
    held = pl.BlockSpec((slot_total, rows, unit), lambda j, k, s, u, c: (0, 0, 2 * u[j] + k))
    passing = pl.BlockSpec((paths, rows, unit), lambda j, k, s, u, c: (0, 0, 2 * j + k))
    leaving = pl.BlockSpec((paths, rows, unit), lambda j, k, s, u, c: (0, 0, skipped + 2 * j + k))
    whole = pl.BlockSpec(memory_space=pl.ANY)
    results = [pltpu.HBM(x.shape, x.dtype) for x in (master, momentum)] if stores else []
    if out_width:
        results.append(pltpu.HBM((paths, rows, out_width), jnp.bfloat16))
    master, momentum, *earlier = [
        pltpu.with_memory_space_constraint(x, pltpu.HBM) for x in (master, momentum, *earlier)
    ]
    return pl.pallas_call(
        functools.partial(update_kernel, stores, out_width > 0),
        grid_spec=pltpu.PrefetchScalarGridSpec(
            num_scalar_prefetch=3,
            grid=(blocks.shape[0], 2),
            in_specs=[passing, held, held] + [whole] * len(earlier),
            out_specs=[held] * (2 * stores) + [leaving] * (out_width > 0),
            scratch_shapes=[pltpu.VMEM((slot_total, rows, unit), jnp.float32)],
        ),
        out_shape=results,
        input_output_aliases={6 + i: i for i in range(len(earlier))},
        compiler_params=pltpu.CompilerParams(vmem_limit_bytes=small_vmem),
        cost_estimate=pl.CostEstimate(
            flops=4 * rec.size,
            bytes_accessed=6 * rec.size + 16 * slot_total * rows * width,
            transcendentals=0,
        ),
    )(slots, blocks, shares, rec, master, momentum, *earlier)


def last_update_kernel(first, slots, blocks, shares, rec, master, momentum, *refs):
    new_master, new_momentum, outgoing, fresh, moved, leaving, sent = refs[3:]
    paths, slot_total, width = rec.shape[0], master.shape[0], rec.shape[2]
    unit = width // 2
    start = pl.multiple_of(blocks[0] * width, width)
    copies = []
    for k in range(2):
        cut = slice(k * unit, (k + 1) * unit)
        fresh[:, :, cut] = jnp.zeros((slot_total, rec.shape[1], unit), jnp.float32)
        for p in range(paths):
            fresh[slots[p], :, cut] += rec[p, :, cut]
        for m in range(slot_total):
            mean = fresh[m, :, cut] * shares[m]
            moved[m, :, cut] = momentum_coef * momentum[m, :, cut] + mean
            fresh[m, :, cut] = master[m, :, cut] - outer_rate * (
                mean + momentum_coef * moved[m, :, cut]
            )
        for p in range(paths):
            leaving[p, :, cut] = fresh[slots[p], :, cut].astype(leaving.dtype)
        for source, target, place in (
            (leaving, outgoing, first + k * unit),
            (fresh, new_master, start + k * unit),
            (moved, new_momentum, start + k * unit),
        ):
            here = pl.ds(pl.multiple_of(place, unit), unit)
            copies.append(
                pltpu.make_async_copy(
                    source.at[:, :, cut], target.at[:, :, here], sent.at[len(copies)]
                )
            )
            copies[-1].start()
    for copy in copies:
        copy.wait()


def last_update(slots, blocks, shares, rec, master, momentum, earlier, first):
    block = (master.shape[0], rec.shape[1], rec.shape[2])
    number, inside = (pl.BlockSpec(memory_space=m) for m in (pltpu.SMEM, pltpu.VMEM))
    whole = pl.BlockSpec(memory_space=pl.ANY)
    rec, master, momentum = [
        pltpu.with_memory_space_constraint(x, pltpu.VMEM) for x in (rec, master, momentum)
    ]
    earlier = [pltpu.with_memory_space_constraint(x, pltpu.HBM) for x in earlier]
    return pl.pallas_call(
        functools.partial(last_update_kernel, first),
        in_specs=[number] * 3 + [inside] * 3 + [whole] * 3,
        out_specs=[whole] * 3,
        out_shape=[pltpu.HBM(x.shape, x.dtype) for x in earlier],
        scratch_shapes=[
            pltpu.VMEM(block, jnp.float32),
            pltpu.VMEM(block, jnp.float32),
            pltpu.VMEM(rec.shape, jnp.bfloat16),
            pltpu.SemaphoreType.DMA((6,)),
        ],
        input_output_aliases={6 + i: i for i in range(3)},
        compiler_params=pltpu.CompilerParams(vmem_limit_bytes=small_vmem),
        cost_estimate=pl.CostEstimate(
            flops=4 * rec.size, bytes_accessed=8 * rec.size, transcendentals=0
        ),
    )(slots, blocks, shares, rec, master, momentum, *earlier)


def place_kernel(orders, which, *refs):
    *pieces, out = refs
    width = out.shape[1] // len(orders[0])
    for choice, order in enumerate(orders):

        @pl.when(which[0] == choice)
        def _():
            k = 0
            for piece in pieces:
                for i in range(piece.shape[1] // width):
                    first = order[k] * width
                    out[:, first : first + width] = piece[:, i * width : (i + 1) * width]
                    k += 1


def place(orders, which, pieces):
    rows, width = pieces[0].shape
    whole = len(orders[0]) * width
    tile = rows // 2
    return pl.pallas_call(
        functools.partial(place_kernel, orders),
        grid_spec=pltpu.PrefetchScalarGridSpec(
            num_scalar_prefetch=1,
            grid=(rows // tile,),
            in_specs=[pl.BlockSpec((tile, p.shape[1]), lambda i, u: (i, 0)) for p in pieces],
            out_specs=pl.BlockSpec((tile, whole), lambda i, u: (i, 0)),
        ),
        out_shape=jax.ShapeDtypeStruct((rows, whole), pieces[0].dtype),
        compiler_params=pltpu.CompilerParams(vmem_limit_bytes=kernel_vmem),
        cost_estimate=pl.CostEstimate(
            flops=0, bytes_accessed=4 * rows * whole, transcendentals=0
        ),
    )(which, *pieces)


def back_kernel(scale, starts, weights, *refs):
    out = refs[-1]
    total = jnp.zeros(out.shape, jnp.float32)
    for i, block in enumerate(refs[:-1]):
        depth = block.shape[1]
        first = pl.multiple_of(starts[i], depth)
        total += jnp.dot(
            block[...], weights[pl.ds(first, depth), :], preferred_element_type=jnp.float32
        )
    out[...] = (total * scale).astype(out.dtype)


def input_gradient(blocks, starts, weights, scale):
    tokens = blocks[0].shape[0]
    model_width, width = weights.shape
    tile = min(tokens, 512)
    return pl.pallas_call(
        functools.partial(back_kernel, scale),
        grid_spec=pltpu.PrefetchScalarGridSpec(
            num_scalar_prefetch=1,
            grid=(tokens // tile,),
            in_specs=[pl.BlockSpec((model_width, width), lambda i, u: (0, 0))]
            + [pl.BlockSpec((tile, b.shape[1]), lambda i, u: (i, 0)) for b in blocks],
            out_specs=pl.BlockSpec((tile, width), lambda i, u: (i, 0)),
        ),
        out_shape=jax.ShapeDtypeStruct((tokens, width), jnp.bfloat16),
        compiler_params=pltpu.CompilerParams(vmem_limit_bytes=kernel_vmem),
        cost_estimate=pl.CostEstimate(
            flops=2 * tokens * model_width * width,
            bytes_accessed=2 * (tokens * model_width + model_width * width + tokens * width),
            transcendentals=0,
        ),
    )(starts, weights, *blocks)


def on_device(
    inputs, out_grad, path_weights, inner_drift, path_module, module_slot, master, momentum
):
    paths = lax.axis_size("path")
    size = lax.axis_size("shard")
    me = lax.axis_index("shard")
    model_width = path_weights.shape[2]
    width = out_grad.shape[1]
    half = width // 2
    rows = master.shape[1]
    slot_total = master.shape[0]
    unit_scale = 1.0 / math.sqrt(model_width)

    here, left, right, far = me, (me + size - 1) % size, (me + 1) % size, (me + 2) % size
    odd = lax.axis_index("path") % 2

    def stepped(block, sense):
        return lax.ppermute(
            block,
            ("path", "shard"),
            [
                (p * size + y, p * size + (y + (sense if p % 2 == 0 else -sense)) % size)
                for p in range(paths)
                for y in range(size)
            ],
        )

    chosen = path_module[:, 0]
    matches = chosen[:, None] == jnp.arange(module_slot.shape[0], dtype=jnp.int32)[None, :]
    slots = jnp.sum(jnp.where(matches, module_slot[None, :], 0), axis=1)
    shares = 1.0 / jnp.sum(
        (slots[None, :] == jnp.arange(slot_total, dtype=jnp.int32)[:, None]).astype(jnp.float32),
        axis=1,
    )

    drift = inner_drift[0]
    turned_inputs = lax.optimization_barrier(inputs.T)

    def drift_columns(block):
        return lax.dynamic_slice(drift, (0, block * width), (drift.shape[0], width))

    def pseudo_pieces(block, moved):
        raw = jnp.dot(turned_inputs, block, preferred_element_type=jnp.float32)
        value = (moved + inner_rate * (raw * unit_scale)) * pseudo_lift
        return value.astype(jnp.float16).reshape(paths, rows, width)

    def exchange(pieces):
        return lax.all_to_all(pieces, "path", split_axis=0, concat_axis=0, tiled=True)

    def received(got):
        return got.astype(jnp.float32) * (1.0 / pseudo_lift)

    def updated(rec, blocks, earlier, **choice):
        order = jnp.stack(blocks).astype(jnp.int32)
        return update(slots, order, shares, rec, master, momentum, earlier, **choice)

    first_block = stepped(out_grad, 1)
    pieces = pseudo_pieces(out_grad, drift_columns(here))
    pieces, late_grad = lax.optimization_barrier((pieces, out_grad))
    second_block = stepped(late_grad, -1)
    got = exchange(pieces)
    *earlier, outgoing = updated(received(got), [here], [], out_width=width)
    own_sent = exchange(outgoing).reshape(paths * rows, width)
    first, second = jnp.where(odd == 0, left, right), jnp.where(odd == 0, right, left)
    far_store = [
        lax.dynamic_slice(store, (0, 0, far * width), (slot_total, rows, width))
        for store in (master, momentum)
    ]
    first_block, own_sent, far_store = lax.optimization_barrier((first_block, own_sent, far_store))
    first_pieces = pseudo_pieces(first_block, drift_columns(first))
    first_block, first_pieces = lax.optimization_barrier((first_block, first_pieces))
    both_pieces = lax.optimization_barrier(jnp.pad(first_pieces, ((0, 0), (0, 0), (0, width))))
    far_block = stepped(first_block, 1)

    second_pieces = pseudo_pieces(second_block, drift_columns(second))
    got = exchange(lax.dynamic_update_slice(both_pieces, second_pieces, (0, 0, width)))
    far_pieces = pseudo_pieces(far_block, drift_columns(far))
    got, far_pieces = lax.optimization_barrier((got, far_pieces))
    far_got = exchange(far_pieces)
    even_path = (jnp.arange(paths) % 2 == 0)[:, None, None]
    left_got = jnp.where(even_path, got[:, :, :width], got[:, :, width:])
    right_got = jnp.where(even_path, got[:, :, width:], got[:, :, :width])
    *earlier, outgoing = updated(
        received(jnp.concatenate([left_got, right_got], axis=2)),
        [left, right],
        earlier,
        out_width=3 * width,
    )
    new_master, new_momentum, outgoing = last_update(
        slots,
        far.astype(jnp.int32)[None],
        shares,
        received(far_got),
        *far_store,
        [*earlier, outgoing],
        2 * width,
    )
    sent = exchange(outgoing).reshape(paths * rows, 3 * width)

    blocks = [out_grad, first_block, second_block, far_block]
    starts = jnp.stack([here, first, second, far]).astype(jnp.int32) * width
    input_grad = input_gradient(blocks, starts, path_weights[0].T, unit_scale)
    sent, new_master, new_momentum, input_grad = lax.optimization_barrier(
        (sent, new_master, new_momentum, input_grad)
    )
    orders = [[(i + d) % size for d in (0, size - 1, 1, 2)] for i in range(size)]
    new_weights = place(orders, me.astype(jnp.int32)[None], [own_sent, sent])
    return (input_grad, new_master, new_momentum, new_weights[None])


def solution(mesh):
    placed = (
        P("path", "shard"),
        P("path", "shard"),
        P("path", "shard", None),
        P("path", "shard", None),
        P(),
        P(),
        P(None, ("shard", "path"), None),
        P(None, ("shard", "path"), None),
    )
    return jax.shard_map(
        on_device,
        mesh=mesh,
        in_specs=placed,
        out_specs=(
            P("path", "shard"),
            P(None, ("shard", "path"), None),
            P(None, ("shard", "path"), None),
            P("path", "shard", None),
        ),
        check_vma=False,
    )
```

```python
import functools
import math

import jax
import jax.numpy as jnp
from jax import lax
from jax.experimental import pallas as pl
from jax.experimental.pallas import tpu as pltpu
from jax.sharding import PartitionSpec as P

inner_rate = 0.5
outer_rate = 0.7
momentum_coef = 0.9
pseudo_lift = 64.0
weight_lift = 32.0
kernel_vmem = 24 * 1024 * 1024
small_vmem = 10 * 1024 * 1024


def update_kernel(stores, passes_on, slots, blocks, shares, rec, master, momentum, *refs):
    *results, total = refs[-(2 * stores + passes_on + 1) :]
    paths, slot_total = rec.shape[0], master.shape[0]
    total[...] = jnp.zeros_like(total)
    for p in range(paths):
        total[slots[p]] += rec[p]
    for m in range(slot_total):
        mean = total[m] * shares[m]
        moved = momentum_coef * momentum[m] + mean
        fresh = master[m] - outer_rate * (mean + momentum_coef * moved)
        total[m] = fresh
        if stores:
            results[0][m] = fresh
            results[1][m] = moved
    if passes_on:
        for p in range(paths):
            results[-1][p] = total[slots[p]].astype(results[-1].dtype)


def update(slots, blocks, shares, rec, master, momentum, earlier, out_width=0, first=0, stores=True):
    paths, rows, width = rec.shape
    slot_total = master.shape[0]
    unit = width // blocks.shape[0] // 2
    skipped = first // unit
    held = pl.BlockSpec((slot_total, rows, unit), lambda j, k, s, u, c: (0, 0, 2 * u[j] + k))
    passing = pl.BlockSpec((paths, rows, unit), lambda j, k, s, u, c: (0, 0, 2 * j + k))
    leaving = pl.BlockSpec((paths, rows, unit), lambda j, k, s, u, c: (0, 0, skipped + 2 * j + k))
    whole = pl.BlockSpec(memory_space=pl.ANY)
    results = [pltpu.HBM(x.shape, x.dtype) for x in (master, momentum)] if stores else []
    if out_width:
        results.append(pltpu.HBM((paths, rows, out_width), jnp.bfloat16))
    master, momentum, *earlier = [
        pltpu.with_memory_space_constraint(x, pltpu.HBM) for x in (master, momentum, *earlier)
    ]
    return pl.pallas_call(
        functools.partial(update_kernel, stores, out_width > 0),
        grid_spec=pltpu.PrefetchScalarGridSpec(
            num_scalar_prefetch=3,
            grid=(blocks.shape[0], 2),
            in_specs=[passing, held, held] + [whole] * len(earlier),
            out_specs=[held] * (2 * stores) + [leaving] * (out_width > 0),
            scratch_shapes=[pltpu.VMEM((slot_total, rows, unit), jnp.float32)],
        ),
        out_shape=results,
        input_output_aliases={6 + i: i for i in range(len(earlier))},
        compiler_params=pltpu.CompilerParams(vmem_limit_bytes=small_vmem),
        cost_estimate=pl.CostEstimate(
            flops=4 * rec.size,
            bytes_accessed=6 * rec.size + 16 * slot_total * rows * width,
            transcendentals=0,
        ),
    )(slots, blocks, shares, rec, master, momentum, *earlier)


def last_update_kernel(first, slots, blocks, shares, rec, master, momentum, *refs):
    new_master, new_momentum, outgoing, fresh, moved, leaving, sent = refs[3:]
    paths, slot_total, width = rec.shape[0], master.shape[0], rec.shape[2]
    unit = width // 2
    start = pl.multiple_of(blocks[0] * width, width)
    copies = []
    for k in range(2):
        cut = slice(k * unit, (k + 1) * unit)
        fresh[:, :, cut] = jnp.zeros((slot_total, rec.shape[1], unit), jnp.float32)
        for p in range(paths):
            fresh[slots[p], :, cut] += rec[p, :, cut]
        for m in range(slot_total):
            mean = fresh[m, :, cut] * shares[m]
            moved[m, :, cut] = momentum_coef * momentum[m, :, cut] + mean
            fresh[m, :, cut] = master[m, :, cut] - outer_rate * (
                mean + momentum_coef * moved[m, :, cut]
            )
        for p in range(paths):
            leaving[p, :, cut] = fresh[slots[p], :, cut].astype(leaving.dtype)
        for source, target, place in (
            (leaving, outgoing, first + k * unit),
            (fresh, new_master, start + k * unit),
            (moved, new_momentum, start + k * unit),
        ):
            here = pl.ds(pl.multiple_of(place, unit), unit)
            copies.append(
                pltpu.make_async_copy(
                    source.at[:, :, cut], target.at[:, :, here], sent.at[len(copies)]
                )
            )
            copies[-1].start()
    for copy in copies:
        copy.wait()


def last_update(slots, blocks, shares, rec, master, momentum, earlier, first):
    block = (master.shape[0], rec.shape[1], rec.shape[2])
    number, inside = (pl.BlockSpec(memory_space=m) for m in (pltpu.SMEM, pltpu.VMEM))
    whole = pl.BlockSpec(memory_space=pl.ANY)
    rec, master, momentum = [
        pltpu.with_memory_space_constraint(x, pltpu.VMEM) for x in (rec, master, momentum)
    ]
    earlier = [pltpu.with_memory_space_constraint(x, pltpu.HBM) for x in earlier]
    return pl.pallas_call(
        functools.partial(last_update_kernel, first),
        in_specs=[number] * 3 + [inside] * 3 + [whole] * 3,
        out_specs=[whole] * 3,
        out_shape=[pltpu.HBM(x.shape, x.dtype) for x in earlier],
        scratch_shapes=[
            pltpu.VMEM(block, jnp.float32),
            pltpu.VMEM(block, jnp.float32),
            pltpu.VMEM(rec.shape, jnp.bfloat16),
            pltpu.SemaphoreType.DMA((6,)),
        ],
        input_output_aliases={6 + i: i for i in range(3)},
        compiler_params=pltpu.CompilerParams(vmem_limit_bytes=small_vmem),
        cost_estimate=pl.CostEstimate(
            flops=4 * rec.size, bytes_accessed=8 * rec.size, transcendentals=0
        ),
    )(slots, blocks, shares, rec, master, momentum, *earlier)


def place_kernel(orders, which, *refs):
    *pieces, out = refs
    width = out.shape[1] // len(orders[0])
    for choice, order in enumerate(orders):

        @pl.when(which[0] == choice)
        def _():
            k = 0
            for piece in pieces:
                for i in range(piece.shape[1] // width):
                    first = order[k] * width
                    out[:, first : first + width] = piece[:, i * width : (i + 1) * width]
                    k += 1


def place(orders, which, pieces):
    rows, width = pieces[0].shape
    whole = len(orders[0]) * width
    tile = rows // 2
    return pl.pallas_call(
        functools.partial(place_kernel, orders),
        grid_spec=pltpu.PrefetchScalarGridSpec(
            num_scalar_prefetch=1,
            grid=(rows // tile,),
            in_specs=[pl.BlockSpec((tile, p.shape[1]), lambda i, u: (i, 0)) for p in pieces],
            out_specs=pl.BlockSpec((tile, whole), lambda i, u: (i, 0)),
        ),
        out_shape=jax.ShapeDtypeStruct((rows, whole), pieces[0].dtype),
        compiler_params=pltpu.CompilerParams(vmem_limit_bytes=kernel_vmem),
        cost_estimate=pl.CostEstimate(
            flops=0, bytes_accessed=4 * rows * whole, transcendentals=0
        ),
    )(which, *pieces)


def back_kernel(scale, starts, weights, *refs):
    out = refs[-1]
    total = jnp.zeros(out.shape, jnp.float32)
    for i, block in enumerate(refs[:-1]):
        depth = block.shape[1]
        first = pl.multiple_of(starts[i], depth)
        total += jnp.dot(
            block[...], weights[pl.ds(first, depth), :], preferred_element_type=jnp.float32
        )
    out[...] = (total * scale).astype(out.dtype)


def input_gradient(blocks, starts, weights, scale):
    tokens = blocks[0].shape[0]
    model_width, width = weights.shape
    tile = min(tokens, 512)
    return pl.pallas_call(
        functools.partial(back_kernel, scale),
        grid_spec=pltpu.PrefetchScalarGridSpec(
            num_scalar_prefetch=1,
            grid=(tokens // tile,),
            in_specs=[pl.BlockSpec((model_width, width), lambda i, u: (0, 0))]
            + [pl.BlockSpec((tile, b.shape[1]), lambda i, u: (i, 0)) for b in blocks],
            out_specs=pl.BlockSpec((tile, width), lambda i, u: (i, 0)),
        ),
        out_shape=jax.ShapeDtypeStruct((tokens, width), jnp.bfloat16),
        compiler_params=pltpu.CompilerParams(vmem_limit_bytes=kernel_vmem),
        cost_estimate=pl.CostEstimate(
            flops=2 * tokens * model_width * width,
            bytes_accessed=2 * (tokens * model_width + model_width * width + tokens * width),
            transcendentals=0,
        ),
    )(starts, weights, *blocks)


def on_device(
    inputs, out_grad, path_weights, inner_drift, path_module, module_slot, master, momentum
):
    paths = lax.axis_size("path")
    size = lax.axis_size("shard")
    me = lax.axis_index("shard")
    model_width = path_weights.shape[2]
    width = out_grad.shape[1]
    half = width // 2
    rows = master.shape[1]
    slot_total = master.shape[0]
    unit_scale = 1.0 / math.sqrt(model_width)

    here, left, right, far = me, (me + size - 1) % size, (me + 1) % size, (me + 2) % size
    odd = lax.axis_index("path") % 2

    def stepped(block, sense):
        return lax.ppermute(
            block,
            ("path", "shard"),
            [
                (p * size + y, p * size + (y + (sense if p % 2 == 0 else -sense)) % size)
                for p in range(paths)
                for y in range(size)
            ],
        )

    chosen = path_module[:, 0]
    matches = chosen[:, None] == jnp.arange(module_slot.shape[0], dtype=jnp.int32)[None, :]
    slots = jnp.sum(jnp.where(matches, module_slot[None, :], 0), axis=1)
    shares = 1.0 / jnp.sum(
        (slots[None, :] == jnp.arange(slot_total, dtype=jnp.int32)[:, None]).astype(jnp.float32),
        axis=1,
    )

    drift = inner_drift[0]
    turned_inputs = lax.optimization_barrier(inputs.T)

    def drift_columns(block):
        return lax.dynamic_slice(drift, (0, block * width), (drift.shape[0], width))

    def pseudo_pieces(block, moved):
        raw = jnp.dot(turned_inputs, block, preferred_element_type=jnp.float32)
        value = (moved + inner_rate * (raw * unit_scale)) * pseudo_lift
        return value.astype(jnp.float16).reshape(paths, rows, width)

    def exchange(pieces):
        return lax.all_to_all(pieces, "path", split_axis=0, concat_axis=0, tiled=True)

    def received(got):
        return got.astype(jnp.float32) * (1.0 / pseudo_lift)

    def updated(rec, blocks, earlier, **choice):
        order = jnp.stack(blocks).astype(jnp.int32)
        return update(slots, order, shares, rec, master, momentum, earlier, **choice)

    first_block = stepped(out_grad, 1)
    pieces = pseudo_pieces(out_grad, drift_columns(here))
    pieces, late_grad = lax.optimization_barrier((pieces, out_grad))
    second_block = stepped(late_grad, -1)
    got = exchange(pieces)
    *earlier, outgoing = updated(received(got), [here], [], out_width=width)
    own_sent = exchange(outgoing).reshape(paths * rows, width)
    first, second = jnp.where(odd == 0, left, right), jnp.where(odd == 0, right, left)
    far_store = [
        lax.dynamic_slice(store, (0, 0, far * width), (slot_total, rows, width))
        for store in (master, momentum)
    ]
    first_block, own_sent, far_store = lax.optimization_barrier((first_block, own_sent, far_store))
    first_pieces = pseudo_pieces(first_block, drift_columns(first))
    first_block, first_pieces = lax.optimization_barrier((first_block, first_pieces))
    far_block = stepped(first_block, 1)

    second_pieces = pseudo_pieces(second_block, drift_columns(second))
    got = exchange(jnp.concatenate([first_pieces, second_pieces], axis=2))
    far_pieces = pseudo_pieces(far_block, drift_columns(far))
    got, far_pieces = lax.optimization_barrier((got, far_pieces))
    far_got = exchange(far_pieces)
    even_path = (jnp.arange(paths) % 2 == 0)[:, None, None]
    left_got = jnp.where(even_path, got[:, :, :width], got[:, :, width:])
    right_got = jnp.where(even_path, got[:, :, width:], got[:, :, :width])
    *earlier, outgoing = updated(
        received(jnp.concatenate([left_got, right_got], axis=2)),
        [left, right],
        earlier,
        out_width=3 * width,
    )
    new_master, new_momentum, outgoing = last_update(
        slots,
        far.astype(jnp.int32)[None],
        shares,
        received(far_got),
        *far_store,
        [*earlier, outgoing],
        2 * width,
    )
    sent = exchange(outgoing).reshape(paths * rows, 3 * width)

    blocks = [out_grad, first_block, second_block, far_block]
    starts = jnp.stack([here, first, second, far]).astype(jnp.int32) * width
    input_grad = input_gradient(blocks, starts, path_weights[0].T, unit_scale)
    sent, new_master, new_momentum, input_grad = lax.optimization_barrier(
        (sent, new_master, new_momentum, input_grad)
    )
    orders = [[(i + d) % size for d in (0, size - 1, 1, 2)] for i in range(size)]
    new_weights = place(orders, me.astype(jnp.int32)[None], [own_sent, sent])
    return (input_grad, new_master, new_momentum, new_weights[None])


def solution(mesh):
    placed = (
        P("path", "shard"),
        P("path", "shard"),
        P("path", "shard", None),
        P("path", "shard", None),
        P(),
        P(),
        P(None, ("shard", "path"), None),
        P(None, ("shard", "path"), None),
    )
    return jax.shard_map(
        on_device,
        mesh=mesh,
        in_specs=placed,
        out_specs=(
            P("path", "shard"),
            P(None, ("shard", "path"), None),
            P(None, ("shard", "path"), None),
            P("path", "shard", None),
        ),
        check_vma=False,
    )
```
